32 devices in a mesh: groups: 2 (over x), expert: 16 (over z, y, core).
Axes of the slice: x: 2, y: 2, z: 4, core: 2. Of those that a mesh axis runs over, the one named last changes fastest.
Arguments:
- tokens: bfloat16 [4096, 4096], P(('groups', 'expert')), parts along dimension 0, may hold values from -6 to 6
- grad_out: bfloat16 [4096, 4096], P(('groups', 'expert')), parts along dimension 0, may hold values from -0.09375 to 0.09375
- expert_ids: int32 [4096, 8], P(('groups', 'expert')), parts along dimension 0, may hold values from 0 to 127, all different within a row; in each aligned block of 128 rows (0 to 127, 128 to 255, ...) at most 10 rows name the same one
- route_weight: int32 [4096, 8], P(('groups', 'expert')), parts along dimension 0, may hold values from 1 to 256
- block_expert: int32 [16], replicated, may hold values from 0 to 1, as said below
- gate_blocks: bfloat16 [16, 4096, 128], P('expert'), may hold values from -0.09375 to 0.09375
- up_blocks: bfloat16 [16, 4096, 128], P('expert'), may hold values from -0.09375 to 0.09375
- down_blocks: bfloat16 [16, 128, 4096], P('expert'), may hold values from -0.1875 to 0.1875
Outputs:
- grad_gate: bfloat16 [32, 4096, 128], P(('groups', 'expert')), parts along dimension 0
- grad_up: bfloat16 [32, 4096, 128], P(('groups', 'expert')), parts along dimension 0
- grad_down: bfloat16 [32, 128, 4096], P(('groups', 'expert')), parts along dimension 0
- route_grad: float32 [4096, 8], P(('groups', 'expert')), parts along dimension 0
The draws below stay inside these ranges and needn't reach their ends.
There are 2 independent parts, one for each index of `groups`. The reference program is written for one: setup_inputs(seed, part) draws one part's arguments, and reference() takes and returns one part's arrays. A program takes and returns all parts, laid end to end along the dimension named above; an argument that names none is the same for every part. Nothing has to cross between parts.
Inputs may be any that keep to these rules, and one draw needn't show every extreme that they name: `expert_ids`: in the rows of one device no expert is named more than 10 times. `block_expert`: each of the experts 0 to 1 holds 4 to 12 blocks; no other expert holds any.
All inputs are finite; a program needn't handle non-finite values.
Results may differ from the reference program's by a relative error of at most 0.0057.
Values may be sent and summed in bfloat16 or wider, within the bound.
A program may use at most 192 MiB of HBM per device.

```python
import math
import jax
import jax.numpy as jnp
import numpy as np
from jax import lax

D = 4096
TOP = 8
EXPERTS = 128
BLK = 128
TOK_DEV = 128
CAP = 10
TOKENS = 2048
BLOCKS = 16
N_EXPERT = 16


def draw_block_expert(key, part):
    key = jax.random.fold_in(key, 11)
    first_key, flip_key, perm_key = jax.random.split(key, 3)
    pairs = BLOCKS // 16
    widths_low = jax.random.randint(first_key, (pairs,), 4, 13).astype(jnp.int32)
    widths_low = widths_low.at[0].set(4)
    flips = jax.random.randint(flip_key, (pairs,), 0, 2).astype(jnp.int32)
    first_width = flips * widths_low + (1 - flips) * (16 - widths_low)
    widths = jnp.stack([first_width, 16 - first_width], axis=1).reshape(-1)
    ends = jnp.cumsum(widths)
    block_pos = jnp.arange(BLOCKS, dtype=jnp.int32)
    owner = jnp.sum((block_pos[:, None] >= ends[None, :]).astype(jnp.int32), axis=1)
    order = jax.random.permutation(perm_key, BLOCKS)
    return owner[order].astype(jnp.int32)


def set_ends(array, key, smallest, high):
    shape = array.shape
    place = [jax.random.randint(jax.random.fold_in(key, axis), (), 0, shape[axis]) for axis in range(len(shape))]
    array = array.at[tuple(place)].set(smallest)
    longest = shape.index(max(shape))
    place[longest] = (place[longest] + 1) % shape[longest]
    return array.at[tuple(place)].set(high)


def levels(stream_key, shape, shards, least, high):
    def one(position, blocks):
        draws = jax.random.uniform(jax.random.fold_in(jax.random.fold_in(stream_key, 6), position), (blocks,), jnp.float32, least / len(shards), high / len(shards))
        return jnp.repeat(jnp.exp(draws), shape[position] // blocks).reshape((-1,) + (1,) * (len(shape) - position - 1))

    factor_of = one(*shards[0])
    for cut in shards[1:]:
        factor_of = factor_of * one(*cut)
    return factor_of


def assign_block(own_key, own, number, rows, number_of, top, bound, skew):
    ranking = jax.random.permutation(own_key, number_of)
    packed, usual = portions_of(number_of, rows * top, bound, skew, True), portions_of(number_of, rows * top, bound, skew, False)
    places = jnp.arange(number_of)

    def named(tallies, turn):
        used = int((tallies > 0).sum())
        fixed = max(1, used // 4)
        passed = fixed + (places - fixed + turn * (used - fixed)) % max(1, number_of - fixed)
        return jnp.zeros((number_of,), jnp.int32).at[ranking[jnp.where(places < fixed, places, passed)]].set(jnp.asarray(tallies, jnp.int32))

    tallies = jnp.where(number % 4 == 0, named(packed, number // 4), named(usual, number - number // 4 - 1))
    mixed = jax.random.permutation(jax.random.fold_in(own, 3), number_of)
    donor, taker = mixed[0:number_of // 2 * 2:2], mixed[1:number_of // 2 * 2:2]
    slack = jnp.minimum(tallies[donor] - 1, bound - tallies[taker]) // 2
    slack = jnp.where((donor == ranking[0]) | (taker == ranking[0]) | (tallies[taker] == 0), 0, jnp.maximum(slack, 0))
    passed = jax.random.randint(jax.random.fold_in(own, 4), (number_of // 2,), 0, 1 << 20) % (slack + 1)
    tallies = tallies.at[donor].add(-passed).at[taker].add(passed)
    labels = jnp.searchsorted(jnp.cumsum(tallies), jnp.arange(rows * top), side="right").astype(jnp.int32)
    listing = labels.reshape(top, rows).T
    listing = listing[jax.random.permutation(jax.random.fold_in(own, 1), rows)]
    turn = jax.random.randint(jax.random.fold_in(own, 2), (rows, 1), 0, top)
    return jnp.take_along_axis(listing, (jnp.arange(top)[None, :] + turn) % top, axis=1)


def portions_of(amount, total, most, lean, full):
    weights = [(1 << 20) // math.isqrt(grade ** lean) + 1 for grade in range(1, amount + 1)]
    largest = most if full else min(most, max(-(-total // amount), total * weights[0] // sum(weights)))
    least = 1 if total - largest >= amount - 1 else 0
    given, surplus = [largest] + [least] * (amount - 1), total - largest - least * (amount - 1)
    while surplus > 0:
        free = [i for i in range(1, amount) if given[i] < largest] or [i for i in range(1, amount) if given[i] < most]
        whole, remaining = sum([weights[i] for i in free]), surplus
        for i in free:
            more = min(most - given[i], max(1, remaining * weights[i] // whole), surplus)
            given[i] = given[i] + more
            surplus = surplus - more
    return np.array(given)


def bell_draw(rng, dims, spread, most, shards=(), held_as=jnp.bfloat16):
    level = levels(rng, dims, shards, -0.22, 0.18) if shards else 1.0
    drawn = jax.random.normal(rng, dims, jnp.float32) * spread * level
    return jnp.minimum(jnp.maximum(drawn, -most), most).astype(held_as)


def setup_inputs(seed: int = 0, part: int = 0) -> dict:
    key_of = jax.random.split(jax.random.key(seed), 9)
    part_splits = jax.random.split(jax.random.fold_in(key_of[8], part), 9)
    tokens = bell_draw(part_splits[0], (TOKENS, D), 1.0, 6.0, ((0, 16),))
    grad_out = bell_draw(part_splits[1], (TOKENS, D), 0.015625, 0.09375, ((0, 16),))
    expert_ids_keys = jax.random.split(jax.random.fold_in(part_splits[2], 1), TOKENS // TOK_DEV)
    expert_ids_turns = jax.random.permutation(jax.random.fold_in(part_splits[2], 3), TOKENS // TOK_DEV)
    expert_ids = jax.vmap(lambda own, number: assign_block(jax.random.fold_in(part_splits[2], 2), own, number, TOK_DEV, EXPERTS, TOP, CAP, 1))(expert_ids_keys, expert_ids_turns).reshape((TOKENS, TOP))
    route_weight = set_ends(jax.random.randint(part_splits[3], (TOKENS, TOP), 1, 257), jax.random.fold_in(part_splits[3], 1), 1, 256).astype(jnp.int32)
    block_expert = draw_block_expert(jax.random.fold_in(key_of[8], 71), part)
    gate_blocks = bell_draw(key_of[5], (BLOCKS, D, BLK), D ** -0.5, 0.09375, ((0, 16),))
    up_blocks = bell_draw(key_of[6], (BLOCKS, D, BLK), D ** -0.5, 0.09375, ((0, 16),))
    down_blocks = bell_draw(key_of[7], (BLOCKS, BLK, D), (8 * BLK) ** -0.5, 0.1875, ((0, 16),))
    return dict(tokens=tokens, grad_out=grad_out, expert_ids=expert_ids, route_weight=route_weight, block_expert=block_expert, gate_blocks=gate_blocks, up_blocks=up_blocks, down_blocks=down_blocks)


def block_grads(rows_x, rows_dy, gains, gate_w, up_w, down_w):
    pre_gate = jnp.dot(rows_x, gate_w, preferred_element_type=jnp.float32)
    pre_up = jnp.dot(rows_x, up_w, preferred_element_type=jnp.float32)
    sigma = jax.nn.sigmoid(pre_gate)
    hidden = (pre_gate * sigma * pre_up).astype(jnp.bfloat16)
    back_proj = lax.dot_general(rows_dy, down_w, (((1,), (1,)), ((), ())), preferred_element_type=jnp.float32)
    partial_dot = jnp.sum(hidden.astype(jnp.float32) * back_proj, axis=1)
    scaled = (gains[:, None] * hidden.astype(jnp.float32)).astype(jnp.bfloat16)
    grad_down = lax.dot_general(scaled, rows_dy, (((0,), (0,)), ((), ())), preferred_element_type=jnp.float32)
    d_hidden = gains[:, None] * back_proj
    d_gate = (d_hidden * pre_up * sigma * (1.0 + pre_gate * (1.0 - sigma))).astype(jnp.bfloat16)
    d_up = (d_hidden * pre_gate * sigma).astype(jnp.bfloat16)
    grad_gate = lax.dot_general(rows_x, d_gate, (((0,), (0,)), ((), ())), preferred_element_type=jnp.float32)
    grad_up = lax.dot_general(rows_x, d_up, (((0,), (0,)), ((), ())), preferred_element_type=jnp.float32)
    return partial_dot, grad_gate.astype(jnp.bfloat16), grad_up.astype(jnp.bfloat16), grad_down.astype(jnp.bfloat16)


def reference(tokens, grad_out, expert_ids, route_weight, block_expert, gate_blocks, up_blocks, down_blocks):
    gains = route_weight.astype(jnp.float32) / 256.0
    row_limit = N_EXPERT * CAP
    positions = jnp.arange(TOP, dtype=jnp.int32)

    def step(carry, block):
        expert = block_expert[block]
        match = expert_ids == expert
        present = jnp.any(match, axis=1)
        count = jnp.sum(present.astype(jnp.int32))
        picked = jnp.nonzero(present, size=row_limit, fill_value=0)[0].astype(jnp.int32)
        valid = jnp.arange(row_limit, dtype=jnp.int32) < count
        column = jnp.sum(positions[None, :] * match.astype(jnp.int32), axis=1)[picked].astype(jnp.int32)
        gain_rows = jnp.where(valid, jnp.sum(gains * match.astype(jnp.float32), axis=1)[picked], 0.0)
        rows_x = jnp.where(valid[:, None], tokens[picked], jnp.zeros((), tokens.dtype))
        rows_dy = jnp.where(valid[:, None], grad_out[picked], jnp.zeros((), grad_out.dtype))
        partial_dot, grad_gate, grad_up, grad_down = block_grads(
            rows_x, rows_dy, gain_rows, gate_blocks[block], up_blocks[block], down_blocks[block])
        carry = carry.at[picked, column].add(jnp.where(valid, partial_dot, 0.0))
        return carry, (grad_gate, grad_up, grad_down)

    start = jnp.zeros((TOKENS, TOP), jnp.float32)
    route_grad, stacked = lax.scan(step, start, jnp.arange(BLOCKS, dtype=jnp.int32))
    return stacked[0], stacked[1], stacked[2], route_grad
```

```python
import functools

import jax
import jax.numpy as jnp
from jax import lax
from jax.experimental import pallas as pl
from jax.experimental.pallas import tpu as pltpu
from jax.sharding import PartitionSpec as P

EXPERTS = 128
CAP = 10


def forward_part(rows_x, joined_w, blk_width):
    joined = jnp.dot(rows_x, joined_w, preferred_element_type=jnp.float32)
    pre_gate = joined[:, :blk_width]
    pre_up = joined[:, blk_width:]
    sigma = jax.nn.sigmoid(pre_gate)
    hidden = (pre_gate * sigma * pre_up).astype(jnp.bfloat16)
    return (pre_gate, pre_up, sigma, hidden)


def backward_part(rows_x, rows_dy, gains, down_w, pre_gate, pre_up, sigma, hidden, blk_width):
    back_proj = lax.dot_general(
        rows_dy, down_w, (((1,), (1,)), ((), ())), preferred_element_type=jnp.float32
    )
    hidden_wide = hidden.astype(jnp.float32)
    partial_dot = jnp.sum(hidden_wide * back_proj, axis=1)
    scaled = (gains[:, None] * hidden_wide).astype(jnp.bfloat16)
    grad_down = lax.dot_general(
        scaled, rows_dy, (((0,), (0,)), ((), ())), preferred_element_type=jnp.float32
    )
    d_hidden = gains[:, None] * back_proj
    d_gate = (d_hidden * pre_up * sigma * (1.0 + pre_gate * (1.0 - sigma))).astype(jnp.bfloat16)
    d_up = (d_hidden * pre_gate * sigma).astype(jnp.bfloat16)
    d_joined = jnp.concatenate([d_gate, d_up], axis=1)
    grad_joined = lax.dot_general(
        rows_x, d_joined, (((0,), (0,)), ((), ())), preferred_element_type=jnp.float32
    )
    grad_gate = grad_joined[:, :blk_width].astype(jnp.bfloat16)
    grad_up = grad_joined[:, blk_width:].astype(jnp.bfloat16)
    return (partial_dot, grad_gate, grad_up, grad_down.astype(jnp.bfloat16))


def per_device(
    tokens, grad_out, expert_ids, route_weight, block_expert, gate_blocks, up_blocks, down_blocks
):
    devices = lax.axis_size("expert")
    tok_rows = tokens.shape[0]
    top_count = expert_ids.shape[1]
    width = tokens.shape[1]
    blk_width = gate_blocks.shape[2]
    flat_ids = expert_ids.reshape(-1)
    expert_range = jnp.arange(EXPERTS, dtype=jnp.int32)
    one_hot = (flat_ids[:, None] == expert_range[None, :]).astype(jnp.int32)
    ranks = jnp.sum(one_hot * jnp.cumsum(one_hot, axis=0), axis=1) - 1
    slot_pos = flat_ids * CAP + ranks
    owners = jnp.arange(tok_rows * top_count, dtype=jnp.int32) // top_count
    slot_tok = jnp.full((EXPERTS * CAP,), tok_rows, jnp.int32).at[slot_pos].set(owners)
    gains = route_weight.reshape(-1).astype(jnp.float32) / 256.0
    slot_gain = jnp.zeros((EXPERTS * CAP,), jnp.float32).at[slot_pos].set(gains)
    dest_tok = slot_tok.reshape(EXPERTS, CAP)[block_expert]
    dest_gain = slot_gain.reshape(EXPERTS, CAP)[block_expert].astype(jnp.bfloat16)
    zero_row = jnp.zeros((1, width), jnp.bfloat16)
    padded_x = jnp.concatenate([tokens, zero_row], axis=0)
    padded_dy = jnp.concatenate([grad_out, zero_row], axis=0)
    send_x = jnp.take(padded_x, dest_tok, axis=0)
    send_dy = jnp.take(padded_dy, dest_tok, axis=0)
    joined_w = jnp.concatenate([gate_blocks[0], up_blocks[0]], axis=1)
    down_w = down_blocks[0]
    row_total = devices * CAP
    recv_x, recv_dy, recv_gain = (
        lax.all_to_all(send_x, "expert", split_axis=0, concat_axis=0, tiled=True),
        lax.all_to_all(send_dy, "expert", split_axis=0, concat_axis=0, tiled=True),
        lax.all_to_all(dest_gain, "expert", split_axis=0, concat_axis=0, tiled=True),
    )
    rows_x = recv_x.reshape(row_total, width)
    pre_gate, pre_up, sigma, hidden = forward_part(rows_x, joined_w, blk_width)
    rows_dy = recv_dy.reshape(row_total, width)
    row_gain = recv_gain.reshape(row_total).astype(jnp.float32)
    partial_dot, grad_gate, grad_up, grad_down = backward_part(
        rows_x, rows_dy, row_gain, down_w, pre_gate, pre_up, sigma, hidden, blk_width
    )
    returned = lax.all_to_all(
        partial_dot.reshape(devices, CAP), "expert", split_axis=0, concat_axis=0, tiled=True
    )
    plan_hot = (block_expert[:, None] == expert_range[None, :]).astype(jnp.float32)
    per_expert = lax.dot_general(
        plan_hot,
        returned,
        (((0,), (0,)), ((), ())),
        precision=lax.Precision.HIGHEST,
        preferred_element_type=jnp.float32,
    )
    route_grad = per_expert[flat_ids, ranks].reshape(tok_rows, top_count)
    return (grad_gate[None], grad_up[None], grad_down[None], route_grad)

ROWS = 16
MESH = pl.DeviceIdType.MESH


def slot_tables(ids, weights):
    count = ids.shape[1]
    earlier = lax.broadcasted_iota(jnp.int32, (count, count), 0)
    later = lax.broadcasted_iota(jnp.int32, (count, count), 1)
    before = (earlier < later).astype(jnp.float32).astype(jnp.bfloat16)
    found, rank, gain = [], [], []
    for expert in range(2):
        hit = (ids == expert).astype(jnp.float32)
        here = jnp.sum(hit, axis=0, keepdims=True)
        wide = jnp.broadcast_to(here, (ROWS, count))
        found.append(wide)
        rank.append(
            jnp.dot(wide.astype(jnp.bfloat16), before, preferred_element_type=jnp.float32).astype(jnp.int32)
        )
        gain.append(jnp.sum(hit * weights.astype(jnp.float32), axis=0, keepdims=True) * (1.0 / 256.0))
    slot = lax.broadcasted_iota(jnp.int32, (ROWS, count), 0)
    first = jnp.where((slot < CAP) & (rank[0] == slot), found[0], 0.0)
    second = jnp.where((slot >= CAP) & (rank[1] == slot - CAP), found[1], 0.0)
    rest = jnp.where(rank[1] == slot % 4 + (ROWS - CAP), found[1], 0.0)
    return first, second, rest, gain, slot


def gather_kernel(pieces, ids_ref, weight_ref, x_ref, dy_ref, out_ref, own, local_sem, send_sem, recv_sem):
    me = lax.axis_index("expert")
    depth = lax.axis_size("expert") // 4
    z, y, core = me // 4, (me // 2) % 2, me % 2
    width = x_ref.shape[1]
    half = width // 2
    step = own.shape[1] // pieces

    def place(zz, yy, cc):
        return zz * 4 + yy * 2 + cc

    targets = (
        (place(z + 1, y, core), z < depth - 1),
        (place(z - 1, y, core), z > 0),
        (place(z, 1 - y, core), None),
        (place(z, y, 1 - core), None),
    )

    def under(condition, action):
        if condition is None:
            action()
        else:
            pl.when(condition)(action)

    barrier = pltpu.get_barrier_semaphore()
    for device, there in targets:
        under(
            there,
            lambda device=device: pl.semaphore_signal(
                barrier, inc=1, device_id={"expert": device}, device_id_type=MESH
            ),
        )

    first, second, rest, gain, slot = slot_tables(ids_ref[...], weight_ref[...])
    main = (first + second).astype(jnp.bfloat16)
    own[:, 0:width] = jnp.dot(main, x_ref[...], preferred_element_type=jnp.float32).astype(jnp.bfloat16)
    own[:, width : 2 * width] = jnp.dot(main, dy_ref[...], preferred_element_type=jnp.float32).astype(jnp.bfloat16)
    total = jnp.zeros((ROWS, half), jnp.float32)
    for quarter in range(4):
        chosen = jnp.where(slot // 4 == quarter, rest, 0.0).astype(jnp.bfloat16)
        source = x_ref if quarter < 2 else dy_ref
        total = total + jnp.dot(
            chosen, source[:, (quarter % 2) * half : (quarter % 2 + 1) * half], preferred_element_type=jnp.float32
        )
    own[:, 2 * width : 2 * width + half] = total.astype(jnp.bfloat16)
    main_gain = jnp.sum(first * gain[0] + second * gain[1], axis=1, keepdims=True)
    rest_gain = jnp.sum(jnp.where(slot < 4, rest * gain[1], 0.0), axis=1, keepdims=True)
    lane = lax.broadcasted_iota(jnp.int32, (ROWS, 128), 1)
    own[:, 2 * width + half :] = jnp.where(lane < 64, main_gain, rest_gain).astype(jnp.bfloat16)

    peers = 2 + (z > 0).astype(jnp.int32) + (z < depth - 1).astype(jnp.int32)
    pl.semaphore_wait(barrier, peers)

    def columns(piece):
        return pl.ds(pl.multiple_of(piece * step, 128), step)

    def copy(shard, piece, way, mine=False):
        block = out_ref.at[shard, :, columns(piece)]
        return pltpu.make_async_remote_copy(
            src_ref=own.at[:, columns(piece)] if mine else block,
            dst_ref=block,
            send_sem=send_sem.at[way, shard, piece],
            recv_sem=recv_sem.at[shard, piece],
            device_id={"expert": targets[way][0]},
            device_id_type=MESH,
        )

    keep = pltpu.make_async_copy(own, out_ref.at[me], local_sem)
    keep.start()

    def each_piece(action):
        def body(piece, carry):
            action(piece)
            return carry

        lax.fori_loop(0, pieces, body, 0)

    def own_sends(method):
        def action(piece):
            for way in (2, 0, 1, 3):
                under(targets[way][1], lambda way=way: getattr(copy(me, piece, way, True), method)())

        each_piece(action)

    def column_shard(shift, way, method):
        shard = place(z + shift, y, core)

        def action(piece):
            if method == "start":
                copy(shard, piece, 2).wait_recv()
            under(targets[way][1], lambda: getattr(copy(shard, piece, way), method)())
            getattr(copy(shard, piece, 2), method)()
            getattr(copy(shard, piece, 3), method)()

        pl.when((z + shift >= 0) & (z + shift < depth))(lambda: each_piece(action))

    def across_shard(shift, method):
        shard = place(z + shift, 1 - y, core)

        def action(piece):
            if method == "start":
                copy(shard, piece, 3).wait_recv()
            getattr(copy(shard, piece, 3), method)()

        pl.when((z + shift >= 0) & (z + shift < depth))(lambda: each_piece(action))

    def everything(method):
        own_sends(method)
        for shift in range(1, depth + 1):
            if shift < depth:
                column_shard(-shift, 0, method)
                column_shard(shift, 1, method)
            if shift == 1:
                across_shard(0, method)
            else:
                across_shard(1 - shift, method)
                across_shard(shift - 1, method)

    everything("start")

    def sibling(number, carry):
        each_piece(lambda piece: copy(number * 2 + 1 - core, piece, 3).wait_recv())
        return carry

    lax.fori_loop(0, depth * 2, sibling, 0)
    keep.wait()
    everything("wait_send")


def block_kernel(expert_ref, packed_ref, gate_ref, up_ref, down_ref, gate_out, up_out, down_out, dots_out):
    width, blk = gate_ref.shape
    half = width // 2
    rows = packed_ref.shape[0]
    expert = expert_ref[0]
    slot = lax.broadcasted_iota(jnp.int32, (rows, 1), 0) % ROWS
    gains = packed_ref[:, 2 * width + half :].astype(jnp.float32)
    owner = (slot >= CAP).astype(jnp.int32)
    main_on = owner == expert
    rest_on = (slot < 4) & (expert == 1)
    rest = packed_ref[:, 2 * width : 2 * width + half]
    across = (((1,), (1,)), ((), ()))
    down = (((0,), (0,)), ((), ()))

    def dot(a, b, dims=(((1,), (0,)), ((), ()))):
        return lax.dot_general(a, b, dims, preferred_element_type=jnp.float32)

    def up_rows(a, amount):
        return pltpu.roll(a, rows - amount, 0)

    joined = jnp.concatenate([gate_ref[...], up_ref[...]], axis=1)
    pre_main = dot(packed_ref[:, :width], joined)
    back_main = dot(packed_ref[:, width : 2 * width], down_ref[...], across)
    pre_rest = dot(rest, joined[:half]) + up_rows(dot(rest, joined[half:]), 4)
    back_rest = up_rows(dot(rest, down_ref[:, :half], across), 8) + up_rows(
        dot(rest, down_ref[:, half:], across), 12
    )

    def middle(pre, back, gain, on):
        gain = jnp.where(on, gain, 0.0)
        pre_gate, pre_up = pre[:, :blk], pre[:, blk:]
        sigma = jax.nn.sigmoid(pre_gate)
        hidden = (pre_gate * sigma * pre_up).astype(jnp.bfloat16).astype(jnp.float32)
        dots = jnp.where(on, jnp.sum(hidden * back, axis=1, keepdims=True), 0.0)
        d_hidden = gain * back
        d_gate = d_hidden * pre_up * sigma * (1.0 + pre_gate * (1.0 - sigma))
        d_up = d_hidden * pre_gate * sigma
        return dots, gain * hidden, jnp.concatenate([d_gate, d_up], axis=1)

    dots_main, scaled_main, d_main = middle(pre_main, back_main, gains[:, 0:1], main_on)
    dots_rest, scaled_rest, d_rest = middle(pre_rest, back_rest, gains[:, 64:65], rest_on)
    lane = lax.broadcasted_iota(jnp.int32, (rows, 128), 1)
    dots_out[...] = jnp.where(lane < 64, dots_main, dots_rest)

    scaled = scaled_main.astype(jnp.bfloat16)
    d_joined = d_main.astype(jnp.bfloat16)
    for part in range(2):
        d_part = pltpu.roll(d_rest, 4 * part, 0) if part else d_rest
        d_part = d_part.astype(jnp.bfloat16)
        scaled_part = pltpu.roll(scaled_rest, 8 + 4 * part, 0).astype(jnp.bfloat16)
        tile = 512
        for start in range(0, half, tile):
            here = slice(part * half + start, part * half + start + tile)
            rest_here = packed_ref[:, 2 * width + start : 2 * width + start + tile]
            grad = dot(packed_ref[:, here], d_joined, down) + dot(rest_here, d_part, down)
            gate_out[here, :] = grad[:, :blk].astype(jnp.bfloat16)
            up_out[here, :] = grad[:, blk:].astype(jnp.bfloat16)
            there = slice(width + here.start, width + here.stop)
            grad_down = dot(scaled, packed_ref[:, there], down) + dot(scaled_part, rest_here, down)
            down_out[:, here] = grad_down.astype(jnp.bfloat16)


def return_kernel(dots_ref, ids_ref, out_ref, held, send_sem, recv_sem):
    devices = lax.axis_size("expert")
    me = lax.axis_index("expert")

    def each_other(action):
        def body(shift, carry):
            action(lax.rem(me + shift, devices))
            return carry

        lax.fori_loop(1, devices, body, 0)

    barrier = pltpu.get_barrier_semaphore()
    each_other(
        lambda device: pl.semaphore_signal(barrier, inc=1, device_id={"expert": device}, device_id_type=MESH)
    )
    pl.semaphore_wait(barrier, devices - 1)

    def copy(device, landing, sender):
        return pltpu.make_async_remote_copy(
            src_ref=dots_ref.at[device],
            dst_ref=held.at[landing],
            send_sem=send_sem.at[device],
            recv_sem=recv_sem.at[sender],
            device_id={"expert": device},
            device_id_type=MESH,
        )

    each_other(lambda device: copy(device, me, me).start())
    ids = ids_ref[...]
    first, second, rest, _, slot = slot_tables(ids, ids)
    held[me] = dots_ref[me]
    each_other(lambda device: copy(device, device, device).wait_recv())
    total = held[0]
    for device in range(1, devices):
        total = total + held[device]
    main, extra = total[:, 0:1], total[:, 64:65]
    low = jnp.sum(first * main, axis=0, keepdims=True)
    high = jnp.sum(second * main + jnp.where(slot < 4, rest * extra, 0.0), axis=0, keepdims=True)
    out_ref[...] = jnp.where(ids == 0, low, jnp.where(ids == 1, high, 0.0))
    each_other(lambda device: copy(device, me, me).wait_send())


def per_device_gathered(
    tokens, grad_out, expert_ids, route_weight, block_expert, gate_blocks, up_blocks, down_blocks
):
    devices = lax.axis_size("expert")
    count, width = tokens.shape
    blk = gate_blocks.shape[2]
    ids, weights = expert_ids.T, route_weight.T
    total = 2 * width + width // 2 + 128
    pieces = 3
    vmem = pl.BlockSpec(memory_space=pltpu.VMEM)
    anywhere = pl.BlockSpec(memory_space=pl.ANY)
    packed = pl.pallas_call(
        functools.partial(gather_kernel, pieces),
        out_shape=jax.ShapeDtypeStruct((devices, ROWS, total), jnp.bfloat16),
        in_specs=[vmem] * 4,
        out_specs=anywhere,
        scratch_shapes=[
            pltpu.VMEM((ROWS, total), jnp.bfloat16),
            pltpu.SemaphoreType.DMA,
            pltpu.SemaphoreType.DMA((4, devices, pieces)),
            pltpu.SemaphoreType.DMA((devices, pieces)),
        ],
        compiler_params=pltpu.CompilerParams(
            collective_id=0, has_side_effects=True, vmem_limit_bytes=32 * 1024 * 1024
        ),
        name="gather_rows",
    )(ids, weights, tokens, grad_out)
    mine = lax.dynamic_slice(block_expert, (lax.axis_index("expert"),), (1,))
    grad_gate, grad_up, grad_down, dots = pl.pallas_call(
        block_kernel,
        out_shape=(
            jax.ShapeDtypeStruct((width, blk), jnp.bfloat16),
            jax.ShapeDtypeStruct((width, blk), jnp.bfloat16),
            jax.ShapeDtypeStruct((blk, width), jnp.bfloat16),
            jax.ShapeDtypeStruct((devices * ROWS, 128), jnp.float32),
        ),
        in_specs=[pl.BlockSpec(memory_space=pltpu.SMEM)] + [vmem] * 4,
        out_specs=(vmem,) * 4,
        compiler_params=pltpu.CompilerParams(vmem_limit_bytes=56 * 1024 * 1024),
        name="block_grads",
    )(mine, packed.reshape(devices * ROWS, total), gate_blocks[0], up_blocks[0], down_blocks[0])
    route_grad = pl.pallas_call(
        return_kernel,
        out_shape=jax.ShapeDtypeStruct(ids.shape, jnp.float32),
        in_specs=[vmem] * 2,
        out_specs=vmem,
        scratch_shapes=[
            pltpu.VMEM((devices, ROWS, 128), jnp.float32),
            pltpu.SemaphoreType.DMA((devices,)),
            pltpu.SemaphoreType.DMA((devices,)),
        ],
        compiler_params=pltpu.CompilerParams(collective_id=1, has_side_effects=True),
        name="return_dots",
    )(dots.reshape(devices, ROWS, 128), ids)
    return (grad_gate[None], grad_up[None], grad_down[None], route_grad.T)


def solution(mesh):
    body = per_device_gathered if mesh.shape["expert"] == 16 else per_device
    return jax.shard_map(
        body,
        mesh=mesh,
        in_specs=(
            P(("groups", "expert"), None),
            P(("groups", "expert"), None),
            P(("groups", "expert"), None),
            P(("groups", "expert"), None),
            P(),
            P("expert", None, None),
            P("expert", None, None),
            P("expert", None, None),
        ),
        out_specs=(
            P(("groups", "expert"), None, None),
            P(("groups", "expert"), None, None),
            P(("groups", "expert"), None, None),
            P(("groups", "expert"), None),
        ),
        check_vma=False,
    )
```

```python
import functools

import jax
import jax.numpy as jnp
from jax import lax
from jax.experimental import pallas as pl
from jax.experimental.pallas import tpu as pltpu
from jax.sharding import PartitionSpec as P

EXPERTS = 128
CAP = 10


def forward_part(rows_x, joined_w, blk_width):
    joined = jnp.dot(rows_x, joined_w, preferred_element_type=jnp.float32)
    pre_gate = joined[:, :blk_width]
    pre_up = joined[:, blk_width:]
    sigma = jax.nn.sigmoid(pre_gate)
    hidden = (pre_gate * sigma * pre_up).astype(jnp.bfloat16)
    return (pre_gate, pre_up, sigma, hidden)


def backward_part(rows_x, rows_dy, gains, down_w, pre_gate, pre_up, sigma, hidden, blk_width):
    back_proj = lax.dot_general(
        rows_dy, down_w, (((1,), (1,)), ((), ())), preferred_element_type=jnp.float32
    )
    hidden_wide = hidden.astype(jnp.float32)
    partial_dot = jnp.sum(hidden_wide * back_proj, axis=1)
    scaled = (gains[:, None] * hidden_wide).astype(jnp.bfloat16)
    grad_down = lax.dot_general(
        scaled, rows_dy, (((0,), (0,)), ((), ())), preferred_element_type=jnp.float32
    )
    d_hidden = gains[:, None] * back_proj
    d_gate = (d_hidden * pre_up * sigma * (1.0 + pre_gate * (1.0 - sigma))).astype(jnp.bfloat16)
    d_up = (d_hidden * pre_gate * sigma).astype(jnp.bfloat16)
    d_joined = jnp.concatenate([d_gate, d_up], axis=1)
    grad_joined = lax.dot_general(
        rows_x, d_joined, (((0,), (0,)), ((), ())), preferred_element_type=jnp.float32
    )
    grad_gate = grad_joined[:, :blk_width].astype(jnp.bfloat16)
    grad_up = grad_joined[:, blk_width:].astype(jnp.bfloat16)
    return (partial_dot, grad_gate, grad_up, grad_down.astype(jnp.bfloat16))


def per_device(
    tokens, grad_out, expert_ids, route_weight, block_expert, gate_blocks, up_blocks, down_blocks
):
    devices = lax.axis_size("expert")
    tok_rows = tokens.shape[0]
    top_count = expert_ids.shape[1]
    width = tokens.shape[1]
    blk_width = gate_blocks.shape[2]
    flat_ids = expert_ids.reshape(-1)
    expert_range = jnp.arange(EXPERTS, dtype=jnp.int32)
    one_hot = (flat_ids[:, None] == expert_range[None, :]).astype(jnp.int32)
    ranks = jnp.sum(one_hot * jnp.cumsum(one_hot, axis=0), axis=1) - 1
    slot_pos = flat_ids * CAP + ranks
    owners = jnp.arange(tok_rows * top_count, dtype=jnp.int32) // top_count
    slot_tok = jnp.full((EXPERTS * CAP,), tok_rows, jnp.int32).at[slot_pos].set(owners)
    gains = route_weight.reshape(-1).astype(jnp.float32) / 256.0
    slot_gain = jnp.zeros((EXPERTS * CAP,), jnp.float32).at[slot_pos].set(gains)
    dest_tok = slot_tok.reshape(EXPERTS, CAP)[block_expert]
    dest_gain = slot_gain.reshape(EXPERTS, CAP)[block_expert].astype(jnp.bfloat16)
    zero_row = jnp.zeros((1, width), jnp.bfloat16)
    padded_x = jnp.concatenate([tokens, zero_row], axis=0)
    padded_dy = jnp.concatenate([grad_out, zero_row], axis=0)
    send_x = jnp.take(padded_x, dest_tok, axis=0)
    send_dy = jnp.take(padded_dy, dest_tok, axis=0)
    joined_w = jnp.concatenate([gate_blocks[0], up_blocks[0]], axis=1)
    down_w = down_blocks[0]
    row_total = devices * CAP
    recv_x, recv_dy, recv_gain = (
        lax.all_to_all(send_x, "expert", split_axis=0, concat_axis=0, tiled=True),
        lax.all_to_all(send_dy, "expert", split_axis=0, concat_axis=0, tiled=True),
        lax.all_to_all(dest_gain, "expert", split_axis=0, concat_axis=0, tiled=True),
    )
    rows_x = recv_x.reshape(row_total, width)
    pre_gate, pre_up, sigma, hidden = forward_part(rows_x, joined_w, blk_width)
    rows_dy = recv_dy.reshape(row_total, width)
    row_gain = recv_gain.reshape(row_total).astype(jnp.float32)
    partial_dot, grad_gate, grad_up, grad_down = backward_part(
        rows_x, rows_dy, row_gain, down_w, pre_gate, pre_up, sigma, hidden, blk_width
    )
    returned = lax.all_to_all(
        partial_dot.reshape(devices, CAP), "expert", split_axis=0, concat_axis=0, tiled=True
    )
    plan_hot = (block_expert[:, None] == expert_range[None, :]).astype(jnp.float32)
    per_expert = lax.dot_general(
        plan_hot,
        returned,
        (((0,), (0,)), ((), ())),
        precision=lax.Precision.HIGHEST,
        preferred_element_type=jnp.float32,
    )
    route_grad = per_expert[flat_ids, ranks].reshape(tok_rows, top_count)
    return (grad_gate[None], grad_up[None], grad_down[None], route_grad)

ROWS = 16
MESH = pl.DeviceIdType.MESH


def slot_tables(ids, weights):
    count = ids.shape[1]
    earlier = lax.broadcasted_iota(jnp.int32, (count, count), 0)
    later = lax.broadcasted_iota(jnp.int32, (count, count), 1)
    before = (earlier < later).astype(jnp.float32).astype(jnp.bfloat16)
    found, rank, gain = [], [], []
    for expert in range(2):
        hit = (ids == expert).astype(jnp.float32)
        here = jnp.sum(hit, axis=0, keepdims=True)
        wide = jnp.broadcast_to(here, (ROWS, count))
        found.append(wide)
        rank.append(
            jnp.dot(wide.astype(jnp.bfloat16), before, preferred_element_type=jnp.float32).astype(jnp.int32)
        )
        gain.append(jnp.sum(hit * weights.astype(jnp.float32), axis=0, keepdims=True) * (1.0 / 256.0))
    slot = lax.broadcasted_iota(jnp.int32, (ROWS, count), 0)
    first = jnp.where((slot < CAP) & (rank[0] == slot), found[0], 0.0)
    second = jnp.where((slot >= CAP) & (rank[1] == slot - CAP), found[1], 0.0)
    rest = jnp.where(rank[1] == slot % 4 + (ROWS - CAP), found[1], 0.0)
    return first, second, rest, gain, slot


def fused_kernel(
    pieces,
    expert_ref,
    ids_ref,
    weight_ref,
    x_hbm,
    dy_hbm,
    gate_hbm,
    up_hbm,
    down_hbm,
    gate_out,
    up_out,
    down_out,
    route_out,
    x_ref,
    dy_ref,
    joined_ref,
    down_ref,
    packed,
    grad_joined,
    grad_down,
    dots,
    held,
    load_sem,
    store_sem,
    send_sem,
    recv_sem,
    dot_send,
    dot_recv,
):
    me = lax.axis_index("expert")
    devices = lax.axis_size("expert")
    depth = devices // 4
    z, y, core = me // 4, (me // 2) % 2, me % 2
    width = x_ref.shape[1]
    blk = down_ref.shape[0]
    half = width // 2
    step = packed.shape[1] // pieces
    last = pieces - 1

    loads = [
        pltpu.make_async_copy(source, target, load_sem.at[number])
        for number, (source, target) in enumerate(
            (
                (x_hbm, x_ref),
                (dy_hbm, dy_ref),
                (gate_hbm, joined_ref.at[:, 0:blk]),
                (up_hbm, joined_ref.at[:, blk : 2 * blk]),
                (down_hbm, down_ref),
            )
        )
    ]
    for load in loads:
        load.start()

    def each_other(action):
        def body(shift, carry):
            action(lax.rem(me + shift, devices))
            return carry

        lax.fori_loop(1, devices, body, 0)

    barrier = pltpu.get_barrier_semaphore()
    each_other(
        lambda device: pl.semaphore_signal(barrier, inc=1, device_id={"expert": device}, device_id_type=MESH)
    )

    def place(zz, yy, cc):
        return zz * 4 + yy * 2 + cc

    targets = (
        (place(z + 1, y, core), z < depth - 1),
        (place(z - 1, y, core), z > 0),
        (place(z, 1 - y, core), None),
        (place(z, y, 1 - core), None),
    )
    partner = z + 1 - 2 * (z % 2)

    def under(condition, action):
        if condition is None:
            action()
        else:
            pl.when(condition)(action)

    def shard_rows(shard):
        return pl.ds(pl.multiple_of(shard * ROWS, ROWS), ROWS)

    first, second, rest_hot, gain, slot = slot_tables(ids_ref[...], weight_ref[...])
    main = (first + second).astype(jnp.bfloat16)
    mine = shard_rows(me)
    main_gain = jnp.sum(first * gain[0] + second * gain[1], axis=1, keepdims=True)
    rest_gain = jnp.sum(jnp.where(slot < 4, rest_hot * gain[1], 0.0), axis=1, keepdims=True)
    lane = lax.broadcasted_iota(jnp.int32, (ROWS, 128), 1)
    packed[mine, 2 * width + half :] = jnp.where(lane < 64, main_gain, rest_gain).astype(jnp.bfloat16)
    loads[0].wait()
    packed[mine, 0:width] = jnp.dot(main, x_ref[...], preferred_element_type=jnp.float32).astype(jnp.bfloat16)
    loads[1].wait()
    packed[mine, width : 2 * width] = jnp.dot(main, dy_ref[...], preferred_element_type=jnp.float32).astype(
        jnp.bfloat16
    )
    total = jnp.zeros((ROWS, half), jnp.float32)
    for quarter in range(4):
        chosen = jnp.where(slot // 4 == quarter, rest_hot, 0.0).astype(jnp.bfloat16)
        source = x_ref if quarter < 2 else dy_ref
        total = total + jnp.dot(
            chosen, source[:, (quarter % 2) * half : (quarter % 2 + 1) * half], preferred_element_type=jnp.float32
        )
    packed[mine, 2 * width : 2 * width + half] = total.astype(jnp.bfloat16)

    pl.semaphore_wait(barrier, devices - 1)

    def copy(shard, piece, way):
        block = packed.at[shard_rows(shard), pl.ds(pl.multiple_of(piece * step, 128), step)]
        return pltpu.make_async_remote_copy(
            src_ref=block,
            dst_ref=block,
            send_sem=send_sem.at[way, shard, piece],
            recv_sem=recv_sem.at[shard, piece],
            device_id={"expert": targets[way][0]},
            device_id_type=MESH,
        )

    def each_piece(action):
        def body(piece, carry):
            action(piece)
            return carry

        lax.fori_loop(0, pieces, body, 0)

    def own_sends(method):
        def action(piece):
            for way in (2, 0, 1, 3):
                under(targets[way][1], lambda way=way: getattr(copy(me, piece, way), method)())

        each_piece(action)

    def column_shard(shift, way, method):
        shard = place(z + shift, y, core)

        def action(piece):
            if method == "start":
                copy(shard, piece, 2).wait_recv()
            under(targets[way][1], lambda: getattr(copy(shard, piece, way), method)())
            pl.when((piece < last) | (z + shift != partner))(lambda: getattr(copy(shard, piece, 2), method)())
            getattr(copy(shard, piece, 3), method)()

        pl.when((z + shift >= 0) & (z + shift < depth))(lambda: each_piece(action))

    def across_shard(shift, method):
        shard = place(z + shift, 1 - y, core)

        def action(piece):
            if method == "start":
                copy(shard, piece, 3).wait_recv()
            if shift == 0:
                pl.when((piece == last) & (z % 2 == 0))(lambda: getattr(copy(shard, piece, 0), method)())
                pl.when((piece == last) & (z % 2 == 1))(lambda: getattr(copy(shard, piece, 1), method)())
            getattr(copy(shard, piece, 3), method)()

        pl.when((z + shift >= 0) & (z + shift < depth))(lambda: each_piece(action))

    def everything(method):
        own_sends(method)
        for shift in range(1, depth + 1):
            if shift < depth:
                column_shard(-shift, 0, method)
                column_shard(shift, 1, method)
            if shift == 1:
                across_shard(0, method)
            else:
                across_shard(1 - shift, method)
                across_shard(shift - 1, method)

    everything("start")

    def sibling(number, carry):
        each_piece(lambda piece: copy(number * 2 + 1 - core, piece, 3).wait_recv())
        return carry

    lax.fori_loop(0, depth * 2, sibling, 0)
    for load in loads[2:]:
        load.wait()

    rows = packed.shape[0]
    expert = expert_ref[me]
    row_slot = lax.broadcasted_iota(jnp.int32, (rows, 1), 0) % ROWS
    gains = packed[:, 2 * width + half :].astype(jnp.float32)
    main_on = (row_slot >= CAP).astype(jnp.int32) == expert
    rest_on = (row_slot < 4) & (expert == 1)
    rest = packed[:, 2 * width : 2 * width + half]
    across = (((1,), (1,)), ((), ()))
    down = (((0,), (0,)), ((), ()))

    def dot(a, b, dims=(((1,), (0,)), ((), ()))):
        return lax.dot_general(a, b, dims, preferred_element_type=jnp.float32)

    def up_rows(a, amount):
        return pltpu.roll(a, rows - amount, 0)

    pre_main = dot(packed[:, :width], joined_ref[...])
    back_main = dot(packed[:, width : 2 * width], down_ref[...], across)
    pre_rest = dot(rest, joined_ref[:half, :]) + up_rows(dot(rest, joined_ref[half:, :]), 4)
    back_rest = up_rows(dot(rest, down_ref[:, :half], across), 8) + up_rows(
        dot(rest, down_ref[:, half:], across), 12
    )

    def middle(pre, back, gain, on):
        gain = jnp.where(on, gain, 0.0)
        pre_gate, pre_up = pre[:, :blk], pre[:, blk:]
        sigma = jax.nn.sigmoid(pre_gate)
        hidden = (pre_gate * sigma * pre_up).astype(jnp.bfloat16).astype(jnp.float32)
        products = jnp.where(on, jnp.sum(hidden * back, axis=1, keepdims=True), 0.0)
        d_hidden = gain * back
        d_gate = d_hidden * pre_up * sigma * (1.0 + pre_gate * (1.0 - sigma))
        d_up = d_hidden * pre_gate * sigma
        return products, gain * hidden, jnp.concatenate([d_gate, d_up], axis=1)

    dots_main, scaled_main, d_main = middle(pre_main, back_main, gains[:, 0:1], main_on)
    dots_rest, scaled_rest, d_rest = middle(pre_rest, back_rest, gains[:, 64:65], rest_on)
    wide_lane = lax.broadcasted_iota(jnp.int32, (rows, 128), 1)
    dots[...] = jnp.where(wide_lane < 64, dots_main, dots_rest).reshape(devices, ROWS, 128)

    def dot_copy(device, landing, sender):
        return pltpu.make_async_remote_copy(
            src_ref=dots.at[device],
            dst_ref=held.at[landing],
            send_sem=dot_send.at[device],
            recv_sem=dot_recv.at[sender],
            device_id={"expert": device},
            device_id_type=MESH,
        )

    each_other(lambda device: dot_copy(device, me, me).start())
    held[me] = dots[me]

    scaled = scaled_main.astype(jnp.bfloat16)
    d_joined = d_main.astype(jnp.bfloat16)
    stores = []
    for part in range(2):
        d_part = pltpu.roll(d_rest, 4 * part, 0) if part else d_rest
        d_part = d_part.astype(jnp.bfloat16)
        scaled_part = pltpu.roll(scaled_rest, 8 + 4 * part, 0).astype(jnp.bfloat16)
        tile = 512
        for start in range(0, half, tile):
            here = slice(part * half + start, part * half + start + tile)
            rest_here = packed[:, 2 * width + start : 2 * width + start + tile]
            grad = dot(packed[:, here], d_joined, down) + dot(rest_here, d_part, down)
            grad_joined[here, :] = grad.astype(jnp.bfloat16)
            there = slice(width + here.start, width + here.stop)
            grad_down[:, here] = (
                dot(scaled, packed[:, there], down) + dot(scaled_part, rest_here, down)
            ).astype(jnp.bfloat16)
        block = pl.ds(part * half, half)
        for number, (source, target) in enumerate(
            (
                (grad_joined.at[block, 0:blk], gate_out.at[block, :]),
                (grad_joined.at[block, blk : 2 * blk], up_out.at[block, :]),
                (grad_down.at[:, block], down_out.at[:, block]),
            )
        ):
            store = pltpu.make_async_copy(source, target, store_sem.at[part * 3 + number])
            store.start()
            stores.append(store)

    each_other(lambda device: dot_copy(device, device, device).wait_recv())
    total = held[0]
    for device in range(1, devices):
        total = total + held[device]
    ids = ids_ref[...]
    first, second, rest_hot, _, slot = slot_tables(ids, ids)
    total_main, extra = total[:, 0:1], total[:, 64:65]
    low = jnp.sum(first * total_main, axis=0, keepdims=True)
    high = jnp.sum(second * total_main + jnp.where(slot < 4, rest_hot * extra, 0.0), axis=0, keepdims=True)
    route_out[...] = jnp.where(ids == 0, low, jnp.where(ids == 1, high, 0.0))
    each_other(lambda device: dot_copy(device, me, me).wait_send())
    everything("wait_send")
    for store in stores:
        store.wait()


def per_device_gathered(
    tokens, grad_out, expert_ids, route_weight, block_expert, gate_blocks, up_blocks, down_blocks
):
    devices = lax.axis_size("expert")
    count, width = tokens.shape
    blk = gate_blocks.shape[2]
    ids, weights = expert_ids.T, route_weight.T
    total = 2 * width + width // 2 + 128
    pieces = 3
    vmem = pl.BlockSpec(memory_space=pltpu.VMEM)
    anywhere = pl.BlockSpec(memory_space=pl.ANY)
    grad_gate, grad_up, grad_down, route_grad = pl.pallas_call(
        functools.partial(fused_kernel, pieces),
        out_shape=(
            jax.ShapeDtypeStruct((width, blk), jnp.bfloat16),
            jax.ShapeDtypeStruct((width, blk), jnp.bfloat16),
            jax.ShapeDtypeStruct((blk, width), jnp.bfloat16),
            jax.ShapeDtypeStruct(ids.shape, jnp.float32),
        ),
        in_specs=[pl.BlockSpec(memory_space=pltpu.SMEM), vmem, vmem] + [anywhere] * 5,
        out_specs=(anywhere, anywhere, anywhere, vmem),
        scratch_shapes=[
            pltpu.VMEM((count, width), jnp.bfloat16),
            pltpu.VMEM((count, width), jnp.bfloat16),
            pltpu.VMEM((width, 2 * blk), jnp.bfloat16),
            pltpu.VMEM((blk, width), jnp.bfloat16),
            pltpu.VMEM((devices * ROWS, total), jnp.bfloat16),
            pltpu.VMEM((width, 2 * blk), jnp.bfloat16),
            pltpu.VMEM((blk, width), jnp.bfloat16),
            pltpu.VMEM((devices, ROWS, 128), jnp.float32),
            pltpu.VMEM((devices, ROWS, 128), jnp.float32),
            pltpu.SemaphoreType.DMA((5,)),
            pltpu.SemaphoreType.DMA((6,)),
            pltpu.SemaphoreType.DMA((4, devices, pieces)),
            pltpu.SemaphoreType.DMA((devices, pieces)),
            pltpu.SemaphoreType.DMA((devices,)),
            pltpu.SemaphoreType.DMA((devices,)),
        ],
        compiler_params=pltpu.CompilerParams(
            collective_id=0, has_side_effects=True, vmem_limit_bytes=58 * 1024 * 1024
        ),
        name="layer_backward",
    )(block_expert, ids, weights, tokens, grad_out, gate_blocks[0], up_blocks[0], down_blocks[0])
    return (grad_gate[None], grad_up[None], grad_down[None], route_grad.T)


def solution(mesh):
    body = per_device_gathered if mesh.shape["expert"] == 16 else per_device
    return jax.shard_map(
        body,
        mesh=mesh,
        in_specs=(
            P(("groups", "expert"), None),
            P(("groups", "expert"), None),
            P(("groups", "expert"), None),
            P(("groups", "expert"), None),
            P(),
            P("expert", None, None),
            P("expert", None, None),
            P("expert", None, None),
        ),
        out_specs=(
            P(("groups", "expert"), None, None),
            P(("groups", "expert"), None, None),
            P(("groups", "expert"), None, None),
            P(("groups", "expert"), None),
        ),
        check_vma=False,
    )
```

```python
import functools

import jax
import jax.numpy as jnp
from jax import lax
from jax.experimental import pallas as pl
from jax.experimental.pallas import tpu as pltpu
from jax.sharding import PartitionSpec as P

EXPERTS = 128
CAP = 10


def forward_part(rows_x, joined_w, blk_width):
    joined = jnp.dot(rows_x, joined_w, preferred_element_type=jnp.float32)
    pre_gate = joined[:, :blk_width]
    pre_up = joined[:, blk_width:]
    sigma = jax.nn.sigmoid(pre_gate)
    hidden = (pre_gate * sigma * pre_up).astype(jnp.bfloat16)
    return (pre_gate, pre_up, sigma, hidden)


def backward_part(rows_x, rows_dy, gains, down_w, pre_gate, pre_up, sigma, hidden, blk_width):
    back_proj = lax.dot_general(
        rows_dy, down_w, (((1,), (1,)), ((), ())), preferred_element_type=jnp.float32
    )
    hidden_wide = hidden.astype(jnp.float32)
    partial_dot = jnp.sum(hidden_wide * back_proj, axis=1)
    scaled = (gains[:, None] * hidden_wide).astype(jnp.bfloat16)
    grad_down = lax.dot_general(
        scaled, rows_dy, (((0,), (0,)), ((), ())), preferred_element_type=jnp.float32
    )
    d_hidden = gains[:, None] * back_proj
    d_gate = (d_hidden * pre_up * sigma * (1.0 + pre_gate * (1.0 - sigma))).astype(jnp.bfloat16)
    d_up = (d_hidden * pre_gate * sigma).astype(jnp.bfloat16)
    d_joined = jnp.concatenate([d_gate, d_up], axis=1)
    grad_joined = lax.dot_general(
        rows_x, d_joined, (((0,), (0,)), ((), ())), preferred_element_type=jnp.float32
    )
    grad_gate = grad_joined[:, :blk_width].astype(jnp.bfloat16)
    grad_up = grad_joined[:, blk_width:].astype(jnp.bfloat16)
    return (partial_dot, grad_gate, grad_up, grad_down.astype(jnp.bfloat16))


def per_device(
    tokens, grad_out, expert_ids, route_weight, block_expert, gate_blocks, up_blocks, down_blocks
):
    devices = lax.axis_size("expert")
    tok_rows = tokens.shape[0]
    top_count = expert_ids.shape[1]
    width = tokens.shape[1]
    blk_width = gate_blocks.shape[2]
    flat_ids = expert_ids.reshape(-1)
    expert_range = jnp.arange(EXPERTS, dtype=jnp.int32)
    one_hot = (flat_ids[:, None] == expert_range[None, :]).astype(jnp.int32)
    ranks = jnp.sum(one_hot * jnp.cumsum(one_hot, axis=0), axis=1) - 1
    slot_pos = flat_ids * CAP + ranks
    owners = jnp.arange(tok_rows * top_count, dtype=jnp.int32) // top_count
    slot_tok = jnp.full((EXPERTS * CAP,), tok_rows, jnp.int32).at[slot_pos].set(owners)
    gains = route_weight.reshape(-1).astype(jnp.float32) / 256.0
    slot_gain = jnp.zeros((EXPERTS * CAP,), jnp.float32).at[slot_pos].set(gains)
    dest_tok = slot_tok.reshape(EXPERTS, CAP)[block_expert]
    dest_gain = slot_gain.reshape(EXPERTS, CAP)[block_expert].astype(jnp.bfloat16)
    zero_row = jnp.zeros((1, width), jnp.bfloat16)
    padded_x = jnp.concatenate([tokens, zero_row], axis=0)
    padded_dy = jnp.concatenate([grad_out, zero_row], axis=0)
    send_x = jnp.take(padded_x, dest_tok, axis=0)
    send_dy = jnp.take(padded_dy, dest_tok, axis=0)
    joined_w = jnp.concatenate([gate_blocks[0], up_blocks[0]], axis=1)
    down_w = down_blocks[0]
    row_total = devices * CAP
    recv_x, recv_dy, recv_gain = (
        lax.all_to_all(send_x, "expert", split_axis=0, concat_axis=0, tiled=True),
        lax.all_to_all(send_dy, "expert", split_axis=0, concat_axis=0, tiled=True),
        lax.all_to_all(dest_gain, "expert", split_axis=0, concat_axis=0, tiled=True),
    )
    rows_x = recv_x.reshape(row_total, width)
    pre_gate, pre_up, sigma, hidden = forward_part(rows_x, joined_w, blk_width)
    rows_dy = recv_dy.reshape(row_total, width)
    row_gain = recv_gain.reshape(row_total).astype(jnp.float32)
    partial_dot, grad_gate, grad_up, grad_down = backward_part(
        rows_x, rows_dy, row_gain, down_w, pre_gate, pre_up, sigma, hidden, blk_width
    )
    returned = lax.all_to_all(
        partial_dot.reshape(devices, CAP), "expert", split_axis=0, concat_axis=0, tiled=True
    )
    plan_hot = (block_expert[:, None] == expert_range[None, :]).astype(jnp.float32)
    per_expert = lax.dot_general(
        plan_hot,
        returned,
        (((0,), (0,)), ((), ())),
        precision=lax.Precision.HIGHEST,
        preferred_element_type=jnp.float32,
    )
    route_grad = per_expert[flat_ids, ranks].reshape(tok_rows, top_count)
    return (grad_gate[None], grad_up[None], grad_down[None], route_grad)

ROWS = 16
MESH = pl.DeviceIdType.MESH


def slot_tables(ids, weights):
    count = ids.shape[1]
    earlier = lax.broadcasted_iota(jnp.int32, (count, count), 0)
    later = lax.broadcasted_iota(jnp.int32, (count, count), 1)
    before = (earlier < later).astype(jnp.float32).astype(jnp.bfloat16)
    found, rank, gain = [], [], []
    for expert in range(2):
        hit = (ids == expert).astype(jnp.float32)
        here = jnp.sum(hit, axis=0, keepdims=True)
        wide = jnp.broadcast_to(here, (ROWS, count))
        found.append(wide)
        rank.append(
            jnp.dot(wide.astype(jnp.bfloat16), before, preferred_element_type=jnp.float32).astype(jnp.int32)
        )
        gain.append(jnp.sum(hit * weights.astype(jnp.float32), axis=0, keepdims=True) * (1.0 / 256.0))
    slot = lax.broadcasted_iota(jnp.int32, (ROWS, count), 0)
    first = jnp.where((slot < CAP) & (rank[0] == slot), found[0], 0.0)
    second = jnp.where((slot >= CAP) & (rank[1] == slot - CAP), found[1], 0.0)
    rest = jnp.where(rank[1] == slot % 4 + (ROWS - CAP), found[1], 0.0)
    return first, second, rest, gain, slot


def fused_kernel(
    pieces,
    expert_ref,
    ids_ref,
    weight_ref,
    x_hbm,
    dy_hbm,
    gate_hbm,
    up_hbm,
    down_hbm,
    gate_out,
    up_out,
    down_out,
    route_out,
    x_ref,
    dy_ref,
    joined_ref,
    down_ref,
    packed,
    grad_joined,
    grad_down,
    sum_joined,
    sum_down,
    dots,
    held,
    load_sem,
    store_sem,
    send_sem,
    recv_sem,
    dot_send,
    dot_recv,
):
    me = lax.axis_index("expert")
    devices = lax.axis_size("expert")
    depth = devices // 4
    z, y, core = me // 4, (me // 2) % 2, me % 2
    width = x_ref.shape[1]
    blk = down_ref.shape[0]
    half = width // 2
    step = packed.shape[1] // pieces
    last = pieces - 1

    loads = [
        pltpu.make_async_copy(source, target, load_sem.at[number])
        for number, (source, target) in enumerate(
            (
                (x_hbm, x_ref),
                (dy_hbm, dy_ref),
                (gate_hbm, joined_ref.at[:, 0:blk]),
                (up_hbm, joined_ref.at[:, blk : 2 * blk]),
                (down_hbm, down_ref),
            )
        )
    ]
    for load in loads:
        load.start()

    def each_other(action):
        def body(shift, carry):
            action(lax.rem(me + shift, devices))
            return carry

        lax.fori_loop(1, devices, body, 0)

    barrier = pltpu.get_barrier_semaphore()
    each_other(
        lambda device: pl.semaphore_signal(barrier, inc=1, device_id={"expert": device}, device_id_type=MESH)
    )

    def place(zz, yy, cc):
        return zz * 4 + yy * 2 + cc

    targets = (
        (place(z + 1, y, core), z < depth - 1),
        (place(z - 1, y, core), z > 0),
        (place(z, 1 - y, core), None),
        (place(z, y, 1 - core), None),
    )
    partner = z + 1 - 2 * (z % 2)

    def under(condition, action):
        if condition is None:
            action()
        else:
            pl.when(condition)(action)

    def position(shard):
        return lax.rem(shard // 2, 2) * (2 * depth) + (shard // 4) * 2 + lax.rem(shard, 2)

    def shard_rows(shard):
        return pl.ds(pl.multiple_of(position(shard) * ROWS, ROWS), ROWS)

    first, second, rest_hot, gain, slot = slot_tables(ids_ref[...], weight_ref[...])
    main = (first + second).astype(jnp.bfloat16)
    mine = shard_rows(me)
    main_gain = jnp.sum(first * gain[0] + second * gain[1], axis=1, keepdims=True)
    rest_gain = jnp.sum(jnp.where(slot < 4, rest_hot * gain[1], 0.0), axis=1, keepdims=True)
    lane = lax.broadcasted_iota(jnp.int32, (ROWS, 128), 1)
    packed[mine, 2 * width + half :] = jnp.where(lane < 64, main_gain, rest_gain).astype(jnp.bfloat16)
    loads[0].wait()
    packed[mine, 0:width] = jnp.dot(main, x_ref[...], preferred_element_type=jnp.float32).astype(jnp.bfloat16)
    loads[1].wait()
    packed[mine, width : 2 * width] = jnp.dot(main, dy_ref[...], preferred_element_type=jnp.float32).astype(
        jnp.bfloat16
    )
    total = jnp.zeros((ROWS, half), jnp.float32)
    for quarter in range(4):
        chosen = jnp.where(slot // 4 == quarter, rest_hot, 0.0).astype(jnp.bfloat16)
        source = x_ref if quarter < 2 else dy_ref
        total = total + jnp.dot(
            chosen, source[:, (quarter % 2) * half : (quarter % 2 + 1) * half], preferred_element_type=jnp.float32
        )
    packed[mine, 2 * width : 2 * width + half] = total.astype(jnp.bfloat16)

    pl.semaphore_wait(barrier, devices - 1)

    def copy(shard, piece, way):
        block = packed.at[shard_rows(shard), pl.ds(pl.multiple_of(piece * step, 128), step)]
        return pltpu.make_async_remote_copy(
            src_ref=block,
            dst_ref=block,
            send_sem=send_sem.at[way, shard, piece],
            recv_sem=recv_sem.at[shard, piece],
            device_id={"expert": targets[way][0]},
            device_id_type=MESH,
        )

    def each_piece(action):
        def body(piece, carry):
            action(piece)
            return carry

        lax.fori_loop(0, pieces, body, 0)

    def own_sends(method):
        def action(piece):
            for way in (2, 0, 1, 3):
                under(targets[way][1], lambda way=way: getattr(copy(me, piece, way), method)())

        each_piece(action)

    def column_shard(shift, way, method):
        shard = place(z + shift, y, core)

        def action(piece):
            if method == "start":
                copy(shard, piece, 2).wait_recv()
            under(targets[way][1], lambda: getattr(copy(shard, piece, way), method)())
            pl.when((piece < last) | (z + shift != partner))(lambda: getattr(copy(shard, piece, 2), method)())
            getattr(copy(shard, piece, 3), method)()

        pl.when((z + shift >= 0) & (z + shift < depth))(lambda: each_piece(action))

    def across_shard(shift, method):
        shard = place(z + shift, 1 - y, core)

        def action(piece):
            if method == "start":
                copy(shard, piece, 3).wait_recv()
            if shift == 0:
                pl.when((piece == last) & (z % 2 == 0))(lambda: getattr(copy(shard, piece, 0), method)())
                pl.when((piece == last) & (z % 2 == 1))(lambda: getattr(copy(shard, piece, 1), method)())
            getattr(copy(shard, piece, 3), method)()

        pl.when((z + shift >= 0) & (z + shift < depth))(lambda: each_piece(action))

    def early(method):
        own_sends(method)
        for shift in range(1, depth):
            column_shard(-shift, 0, method)
            column_shard(shift, 1, method)
            if shift == 1:
                across_shard(0, method)
            elif shift < depth - 1:
                across_shard(1 - shift, method)
                across_shard(shift - 1, method)

    def late(method):
        for shift in range(depth - 2, depth):
            across_shard(-shift, method)
            across_shard(shift, method)

    def sibling(column):
        def body(number, carry):
            each_piece(lambda piece: copy(place(number, column, 1 - core), piece, 3).wait_recv())
            return carry

        lax.fori_loop(0, depth, body, 0)

    count = packed.shape[0] // 2
    expert = expert_ref[me]
    row_slot = lax.broadcasted_iota(jnp.int32, (count, 1), 0) % ROWS
    main_on = (row_slot >= CAP).astype(jnp.int32) == expert
    rest_on = (row_slot < 4) & (expert == 1)
    on = jnp.concatenate([main_on.astype(jnp.float32), rest_on.astype(jnp.float32)], axis=0) > 0.5
    across = (((1,), (1,)), ((), ()))
    down = (((0,), (0,)), ((), ()))

    def dot(a, b, dims=(((1,), (0,)), ((), ()))):
        return lax.dot_general(a, b, dims, preferred_element_type=jnp.float32)

    def up_rows(a, amount):
        return pltpu.roll(a, count - amount, 0)

    def dot_copy(device, landing, sender):
        return pltpu.make_async_remote_copy(
            src_ref=dots.at[position(device)],
            dst_ref=held.at[landing],
            send_sem=dot_send.at[device],
            recv_sem=dot_recv.at[sender],
            device_id={"expert": device},
            device_id_type=MESH,
        )

    def half_rows(column, finish):
        rows = pl.ds(pl.multiple_of(column * count, count), count)
        rest = packed[rows, 2 * width : 2 * width + half]

        def stacked(start, size, rest_start):
            return jnp.concatenate(
                [packed[rows, start : start + size], rest[:, rest_start : rest_start + size]], axis=0
            )

        pre_low = dot(stacked(0, half, 0), joined_ref[:half, :])
        pre_high = dot(stacked(half, half, 0), joined_ref[half:, :])
        back_low = dot(stacked(width, half, 0), down_ref[:, :half], across)
        back_high = dot(stacked(width + half, half, 0), down_ref[:, half:], across)
        pre = jnp.concatenate(
            [pre_low[:count] + pre_high[:count], pre_low[count:] + up_rows(pre_high[count:], 4)], axis=0
        )
        back = jnp.concatenate(
            [
                back_low[:count] + back_high[:count],
                up_rows(back_low[count:], 8) + up_rows(back_high[count:], 12),
            ],
            axis=0,
        )
        gains = packed[rows, 2 * width + half :].astype(jnp.float32)
        gain = jnp.where(on, jnp.concatenate([gains[:, 0:1], gains[:, 64:65]], axis=0), 0.0)
        pre_gate, pre_up = pre[:, :blk], pre[:, blk:]
        sigma = jax.nn.sigmoid(pre_gate)
        hidden = (pre_gate * sigma * pre_up).astype(jnp.bfloat16).astype(jnp.float32)
        products = jnp.where(on, jnp.sum(hidden * back, axis=1, keepdims=True), 0.0)
        scaled = gain * hidden
        d_hidden = gain * back
        d_gate = d_hidden * pre_up * sigma * (1.0 + pre_gate * (1.0 - sigma))
        d_up = d_hidden * pre_gate * sigma
        d_joined = jnp.concatenate([d_gate, d_up], axis=1)
        wide_lane = lax.broadcasted_iota(jnp.int32, (count, 128), 1)
        dots[pl.ds(column * 2 * depth, 2 * depth)] = jnp.where(
            wide_lane < 64, products[:count], products[count:]
        ).reshape(2 * depth, ROWS, 128)

        def send(number, carry):
            device = place(number // 2, column, lax.rem(number, 2))
            pl.when(device != me)(lambda: dot_copy(device, me, me).start())
            return carry

        lax.fori_loop(0, 2 * depth, send, 0)

        stores = []
        for part in range(2):
            d_rest = pltpu.roll(d_joined[count:], 4 * part, 0) if part else d_joined[count:]
            d_rows = jnp.concatenate([d_joined[:count], d_rest], axis=0).astype(jnp.bfloat16)
            scaled_rows = jnp.concatenate(
                [scaled[:count], pltpu.roll(scaled[count:], 8 + 4 * part, 0)], axis=0
            ).astype(jnp.bfloat16)
            tile = 512
            for start in range(0, half, tile):
                at = part * half + start
                here = slice(at, at + tile)
                grad = dot(stacked(at, tile, start), d_rows, down)
                grad_d = dot(scaled_rows, stacked(width + at, tile, start), down)
                if finish:
                    grad_joined[here, :] = (sum_joined[here, :] + grad).astype(jnp.bfloat16)
                    grad_down[:, here] = (sum_down[:, here] + grad_d).astype(jnp.bfloat16)
                else:
                    sum_joined[here, :] = grad
                    sum_down[:, here] = grad_d
            if finish:
                block = pl.ds(part * half, half)
                for number, (source, target) in enumerate(
                    (
                        (grad_joined.at[block, 0:blk], gate_out.at[block, :]),
                        (grad_joined.at[block, blk : 2 * blk], up_out.at[block, :]),
                        (grad_down.at[:, block], down_out.at[:, block]),
                    )
                ):
                    store = pltpu.make_async_copy(source, target, store_sem.at[part * 3 + number])
                    store.start()
                    stores.append(store)
        return stores

    early("start")
    for load in loads[2:]:
        load.wait()
    sibling(y)
    half_rows(y, False)
    held[me] = dots[position(me)]
    late("start")
    sibling(1 - y)
    stores = half_rows(1 - y, True)

    each_other(lambda device: dot_copy(device, device, device).wait_recv())
    total = held[0]
    for device in range(1, devices):
        total = total + held[device]
    ids = ids_ref[...]
    first, second, rest_hot, _, slot = slot_tables(ids, ids)
    total_main, extra = total[:, 0:1], total[:, 64:65]
    low = jnp.sum(first * total_main, axis=0, keepdims=True)
    high = jnp.sum(second * total_main + jnp.where(slot < 4, rest_hot * extra, 0.0), axis=0, keepdims=True)
    route_out[...] = jnp.where(ids == 0, low, jnp.where(ids == 1, high, 0.0))
    each_other(lambda device: dot_copy(device, me, me).wait_send())
    early("wait_send")
    late("wait_send")
    for store in stores:
        store.wait()


def write_kernel(a_in, b_in, c_in, route_in, a_out, b_out, c_out, route_out, a, b, c, load_sem, store_sem):
    loads, stores = [], []
    for number, (source, through, target) in enumerate(((a_in, a, a_out), (b_in, b, b_out), (c_in, c, c_out))):
        rows = source.shape[0] // 2
        for part in range(2):
            block = pl.ds(part * rows, rows)
            loads.append(
                pltpu.make_async_copy(source.at[block], through.at[block], load_sem.at[number, part])
            )
            stores.append(
                pltpu.make_async_copy(through.at[block], target.at[block], store_sem.at[number, part])
            )
    for load in loads:
        load.start()
    route_out[...] = route_in[...]
    for load, store in zip(loads, stores):
        load.wait()
        store.start()
    for store in stores:
        store.wait()


def per_device_gathered(
    tokens, grad_out, expert_ids, route_weight, block_expert, gate_blocks, up_blocks, down_blocks
):
    devices = lax.axis_size("expert")
    count, width = tokens.shape
    blk = gate_blocks.shape[2]
    ids, weights = expert_ids.T, route_weight.T
    total = 2 * width + width // 2 + 128
    pieces = 3
    vmem = pl.BlockSpec(memory_space=pltpu.VMEM)
    anywhere = pl.BlockSpec(memory_space=pl.ANY)
    grad_gate, grad_up, grad_down, route_grad = pl.pallas_call(
        functools.partial(fused_kernel, pieces),
        out_shape=(
            jax.ShapeDtypeStruct((width, blk), jnp.bfloat16),
            jax.ShapeDtypeStruct((width, blk), jnp.bfloat16),
            jax.ShapeDtypeStruct((blk, width), jnp.bfloat16),
            jax.ShapeDtypeStruct(ids.shape, jnp.float32),
        ),
        in_specs=[pl.BlockSpec(memory_space=pltpu.SMEM), vmem, vmem] + [anywhere] * 5,
        out_specs=(anywhere, anywhere, anywhere, vmem),
        scratch_shapes=[
            pltpu.VMEM((count, width), jnp.bfloat16),
            pltpu.VMEM((count, width), jnp.bfloat16),
            pltpu.VMEM((width, 2 * blk), jnp.bfloat16),
            pltpu.VMEM((blk, width), jnp.bfloat16),
            pltpu.VMEM((devices * ROWS, total), jnp.bfloat16),
            pltpu.VMEM((width, 2 * blk), jnp.bfloat16),
            pltpu.VMEM((blk, width), jnp.bfloat16),
            pltpu.VMEM((width, 2 * blk), jnp.float32),
            pltpu.VMEM((blk, width), jnp.float32),
            pltpu.VMEM((devices, ROWS, 128), jnp.float32),
            pltpu.VMEM((devices, ROWS, 128), jnp.float32),
            pltpu.SemaphoreType.DMA((5,)),
            pltpu.SemaphoreType.DMA((6,)),
            pltpu.SemaphoreType.DMA((4, devices, pieces)),
            pltpu.SemaphoreType.DMA((devices, pieces)),
            pltpu.SemaphoreType.DMA((devices,)),
            pltpu.SemaphoreType.DMA((devices,)),
        ],
        compiler_params=pltpu.CompilerParams(
            collective_id=0, has_side_effects=True, vmem_limit_bytes=58 * 1024 * 1024
        ),
        name="layer_backward",
    )(block_expert, ids, weights, tokens, grad_out, gate_blocks[0], up_blocks[0], down_blocks[0])
    results = (grad_gate, grad_up, grad_down)
    grad_gate, grad_up, grad_down, route_grad = pl.pallas_call(
        write_kernel,
        out_shape=tuple(jax.ShapeDtypeStruct(a.shape, a.dtype) for a in (*results, route_grad)),
        in_specs=[anywhere] * 3 + [vmem],
        out_specs=(anywhere,) * 3 + (vmem,),
        scratch_shapes=[pltpu.VMEM(a.shape, a.dtype) for a in results]
        + [pltpu.SemaphoreType.DMA((3, 2)), pltpu.SemaphoreType.DMA((3, 2))],
        compiler_params=pltpu.CompilerParams(vmem_limit_bytes=58 * 1024 * 1024),
        name="write_results",
    )(*results, route_grad)
    return (grad_gate[None], grad_up[None], grad_down[None], route_grad.T)


def solution(mesh):
    body = per_device_gathered if mesh.shape["expert"] == 16 else per_device
    return jax.shard_map(
        body,
        mesh=mesh,
        in_specs=(
            P(("groups", "expert"), None),
            P(("groups", "expert"), None),
            P(("groups", "expert"), None),
            P(("groups", "expert"), None),
            P(),
            P("expert", None, None),
            P("expert", None, None),
            P("expert", None, None),
        ),
        out_specs=(
            P(("groups", "expert"), None, None),
            P(("groups", "expert"), None, None),
            P(("groups", "expert"), None, None),
            P(("groups", "expert"), None),
        ),
        check_vma=False,
    )
```

```python
import functools

import jax
import jax.numpy as jnp
from jax import lax
from jax.experimental import pallas as pl
from jax.experimental.pallas import tpu as pltpu
from jax.sharding import PartitionSpec as P

EXPERTS = 128
CAP = 10


def forward_part(rows_x, joined_w, blk_width):
    joined = jnp.dot(rows_x, joined_w, preferred_element_type=jnp.float32)
    pre_gate = joined[:, :blk_width]
    pre_up = joined[:, blk_width:]
    sigma = jax.nn.sigmoid(pre_gate)
    hidden = (pre_gate * sigma * pre_up).astype(jnp.bfloat16)
    return (pre_gate, pre_up, sigma, hidden)


def backward_part(rows_x, rows_dy, gains, down_w, pre_gate, pre_up, sigma, hidden, blk_width):
    back_proj = lax.dot_general(
        rows_dy, down_w, (((1,), (1,)), ((), ())), preferred_element_type=jnp.float32
    )
    hidden_wide = hidden.astype(jnp.float32)
    partial_dot = jnp.sum(hidden_wide * back_proj, axis=1)
    scaled = (gains[:, None] * hidden_wide).astype(jnp.bfloat16)
    grad_down = lax.dot_general(
        scaled, rows_dy, (((0,), (0,)), ((), ())), preferred_element_type=jnp.float32
    )
    d_hidden = gains[:, None] * back_proj
    d_gate = (d_hidden * pre_up * sigma * (1.0 + pre_gate * (1.0 - sigma))).astype(jnp.bfloat16)
    d_up = (d_hidden * pre_gate * sigma).astype(jnp.bfloat16)
    d_joined = jnp.concatenate([d_gate, d_up], axis=1)
    grad_joined = lax.dot_general(
        rows_x, d_joined, (((0,), (0,)), ((), ())), preferred_element_type=jnp.float32
    )
    grad_gate = grad_joined[:, :blk_width].astype(jnp.bfloat16)
    grad_up = grad_joined[:, blk_width:].astype(jnp.bfloat16)
    return (partial_dot, grad_gate, grad_up, grad_down.astype(jnp.bfloat16))


def per_device(
    tokens, grad_out, expert_ids, route_weight, block_expert, gate_blocks, up_blocks, down_blocks
):
    devices = lax.axis_size("expert")
    tok_rows = tokens.shape[0]
    top_count = expert_ids.shape[1]
    width = tokens.shape[1]
    blk_width = gate_blocks.shape[2]
    flat_ids = expert_ids.reshape(-1)
    expert_range = jnp.arange(EXPERTS, dtype=jnp.int32)
    one_hot = (flat_ids[:, None] == expert_range[None, :]).astype(jnp.int32)
    ranks = jnp.sum(one_hot * jnp.cumsum(one_hot, axis=0), axis=1) - 1
    slot_pos = flat_ids * CAP + ranks
    owners = jnp.arange(tok_rows * top_count, dtype=jnp.int32) // top_count
    slot_tok = jnp.full((EXPERTS * CAP,), tok_rows, jnp.int32).at[slot_pos].set(owners)
    gains = route_weight.reshape(-1).astype(jnp.float32) / 256.0
    slot_gain = jnp.zeros((EXPERTS * CAP,), jnp.float32).at[slot_pos].set(gains)
    dest_tok = slot_tok.reshape(EXPERTS, CAP)[block_expert]
    dest_gain = slot_gain.reshape(EXPERTS, CAP)[block_expert].astype(jnp.bfloat16)
    zero_row = jnp.zeros((1, width), jnp.bfloat16)
    padded_x = jnp.concatenate([tokens, zero_row], axis=0)
    padded_dy = jnp.concatenate([grad_out, zero_row], axis=0)
    send_x = jnp.take(padded_x, dest_tok, axis=0)
    send_dy = jnp.take(padded_dy, dest_tok, axis=0)
    joined_w = jnp.concatenate([gate_blocks[0], up_blocks[0]], axis=1)
    down_w = down_blocks[0]
    row_total = devices * CAP
    recv_x, recv_dy, recv_gain = (
        lax.all_to_all(send_x, "expert", split_axis=0, concat_axis=0, tiled=True),
        lax.all_to_all(send_dy, "expert", split_axis=0, concat_axis=0, tiled=True),
        lax.all_to_all(dest_gain, "expert", split_axis=0, concat_axis=0, tiled=True),
    )
    rows_x = recv_x.reshape(row_total, width)
    pre_gate, pre_up, sigma, hidden = forward_part(rows_x, joined_w, blk_width)
    rows_dy = recv_dy.reshape(row_total, width)
    row_gain = recv_gain.reshape(row_total).astype(jnp.float32)
    partial_dot, grad_gate, grad_up, grad_down = backward_part(
        rows_x, rows_dy, row_gain, down_w, pre_gate, pre_up, sigma, hidden, blk_width
    )
    returned = lax.all_to_all(
        partial_dot.reshape(devices, CAP), "expert", split_axis=0, concat_axis=0, tiled=True
    )
    plan_hot = (block_expert[:, None] == expert_range[None, :]).astype(jnp.float32)
    per_expert = lax.dot_general(
        plan_hot,
        returned,
        (((0,), (0,)), ((), ())),
        precision=lax.Precision.HIGHEST,
        preferred_element_type=jnp.float32,
    )
    route_grad = per_expert[flat_ids, ranks].reshape(tok_rows, top_count)
    return (grad_gate[None], grad_up[None], grad_down[None], route_grad)

ROWS = 16
MESH = pl.DeviceIdType.MESH


def slot_tables(ids, weights):
    count = ids.shape[1]
    earlier = lax.broadcasted_iota(jnp.int32, (count, count), 0)
    later = lax.broadcasted_iota(jnp.int32, (count, count), 1)
    before = (earlier < later).astype(jnp.float32).astype(jnp.bfloat16)
    found, rank, gain = [], [], []
    for expert in range(2):
        hit = (ids == expert).astype(jnp.float32)
        here = jnp.sum(hit, axis=0, keepdims=True)
        wide = jnp.broadcast_to(here, (ROWS, count))
        found.append(wide)
        rank.append(
            jnp.dot(wide.astype(jnp.bfloat16), before, preferred_element_type=jnp.float32).astype(jnp.int32)
        )
        gain.append(jnp.sum(hit * weights.astype(jnp.float32), axis=0, keepdims=True) * (1.0 / 256.0))
    slot = lax.broadcasted_iota(jnp.int32, (ROWS, count), 0)
    first = jnp.where((slot < CAP) & (rank[0] == slot), found[0], 0.0)
    second = jnp.where((slot >= CAP) & (rank[1] == slot - CAP), found[1], 0.0)
    rest = jnp.where(rank[1] == slot % 4 + (ROWS - CAP), found[1], 0.0)
    return first, second, rest, gain, slot


def fused_kernel(
    pieces,
    expert_ref,
    ids_ref,
    weight_ref,
    x_hbm,
    dy_hbm,
    gate_hbm,
    up_hbm,
    down_hbm,
    gate_out,
    up_out,
    down_out,
    route_out,
    x_ref,
    dy_ref,
    joined_ref,
    down_ref,
    packed,
    grad_joined,
    grad_down,
    sum_joined,
    sum_down,
    dots,
    held,
    load_sem,
    store_sem,
    send_sem,
    recv_sem,
    dot_send,
    dot_recv,
):
    me = lax.axis_index("expert")
    devices = lax.axis_size("expert")
    depth = devices // 4
    z, y, core = me // 4, (me // 2) % 2, me % 2
    width = x_ref.shape[1]
    blk = down_ref.shape[0]
    half = width // 2
    step = packed.shape[1] // pieces

    loads = [
        pltpu.make_async_copy(source, target, load_sem.at[number])
        for number, (source, target) in enumerate(
            (
                (x_hbm, x_ref),
                (dy_hbm, dy_ref),
                (gate_hbm, joined_ref.at[:, 0:blk]),
                (up_hbm, joined_ref.at[:, blk : 2 * blk]),
                (down_hbm, down_ref),
            )
        )
    ]
    for load in loads:
        load.start()

    def each_other(action):
        def body(shift, carry):
            action(lax.rem(me + shift, devices))
            return carry

        lax.fori_loop(1, devices, body, 0)

    barrier = pltpu.get_barrier_semaphore()
    each_other(
        lambda device: pl.semaphore_signal(barrier, inc=1, device_id={"expert": device}, device_id_type=MESH)
    )

    def place(zz, yy, cc):
        return zz * 4 + yy * 2 + cc

    targets = (
        (place(z + 1, y, core), z < depth - 1),
        (place(z - 1, y, core), z > 0),
        (place(z, 1 - y, core), None),
        (place(z, y, 1 - core), None),
    )

    def under(condition, action):
        if condition is None:
            action()
        else:
            pl.when(condition)(action)

    def position(shard):
        return lax.rem(shard // 2, 2) * (2 * depth) + (shard // 4) * 2 + lax.rem(shard, 2)

    def shard_rows(shard):
        return pl.ds(pl.multiple_of(position(shard) * ROWS, ROWS), ROWS)

    first, second, rest_hot, gain, slot = slot_tables(ids_ref[...], weight_ref[...])
    main = (first + second).astype(jnp.bfloat16)
    mine = shard_rows(me)
    main_gain = jnp.sum(first * gain[0] + second * gain[1], axis=1, keepdims=True)
    rest_gain = jnp.sum(jnp.where(slot < 4, rest_hot * gain[1], 0.0), axis=1, keepdims=True)
    lane = lax.broadcasted_iota(jnp.int32, (ROWS, 128), 1)
    packed[mine, 2 * width + half :] = jnp.where(lane < 64, main_gain, rest_gain).astype(jnp.bfloat16)
    loads[0].wait()
    packed[mine, 0:width] = jnp.dot(main, x_ref[...], preferred_element_type=jnp.float32).astype(jnp.bfloat16)
    pl.semaphore_wait(barrier, devices - 1)

    def copy(shard, piece, way):
        block = packed.at[shard_rows(shard), pl.ds(pl.multiple_of(piece * step, 128), step)]
        return pltpu.make_async_remote_copy(
            src_ref=block,
            dst_ref=block,
            send_sem=send_sem.at[way, shard, piece],
            recv_sem=recv_sem.at[shard, piece],
            device_id={"expert": targets[way][0]},
            device_id_type=MESH,
        )

    def each_piece(action):
        def body(piece, carry):
            action(piece)
            return carry

        lax.fori_loop(0, pieces, body, 0)

    def own_piece(piece, method):
        for way in (2, 0, 1, 3):
            under(targets[way][1], lambda way=way: getattr(copy(me, piece, way), method)())

    own_piece(0, "start")
    loads[1].wait()
    packed[mine, width : 2 * width] = jnp.dot(main, dy_ref[...], preferred_element_type=jnp.float32).astype(
        jnp.bfloat16
    )
    total = jnp.zeros((ROWS, half), jnp.float32)
    for quarter in range(4):
        chosen = jnp.where(slot // 4 == quarter, rest_hot, 0.0).astype(jnp.bfloat16)
        source = x_ref if quarter < 2 else dy_ref
        total = total + jnp.dot(
            chosen, source[:, (quarter % 2) * half : (quarter % 2 + 1) * half], preferred_element_type=jnp.float32
        )
    packed[mine, 2 * width : 2 * width + half] = total.astype(jnp.bfloat16)
    for piece in range(1, pieces):
        own_piece(piece, "start")

    def column_shard(shift, way, method):
        shard = place(z + shift, y, core)

        def action(piece):
            if method == "start":
                copy(shard, piece, 2).wait_recv()
            under(targets[way][1], lambda: getattr(copy(shard, piece, way), method)())
            getattr(copy(shard, piece, 2), method)()
            getattr(copy(shard, piece, 3), method)()

        pl.when((z + shift >= 0) & (z + shift < depth))(lambda: each_piece(action))

    def across_shard(shift, method):
        shard = place(z + shift, 1 - y, core)

        def action(piece):
            if method == "start":
                copy(shard, piece, 3).wait_recv()
            getattr(copy(shard, piece, 3), method)()

        pl.when((z + shift >= 0) & (z + shift < depth))(lambda: each_piece(action))

    def early(method):
        for shift in range(1, depth):
            column_shard(-shift, 0, method)
            column_shard(shift, 1, method)
            if shift == 1:
                across_shard(0, method)
            elif shift < depth - 1:
                across_shard(1 - shift, method)
                across_shard(shift - 1, method)

    def late(method):
        for shift in range(depth - 2, depth):
            across_shard(-shift, method)
            across_shard(shift, method)

    def sibling(column):
        def body(number, carry):
            each_piece(lambda piece: copy(place(number, column, 1 - core), piece, 3).wait_recv())
            return carry

        lax.fori_loop(0, depth, body, 0)

    count = packed.shape[0] // 2
    expert = expert_ref[me]
    row_slot = lax.broadcasted_iota(jnp.int32, (count, 1), 0) % ROWS
    main_on = (row_slot >= CAP).astype(jnp.int32) == expert
    rest_on = (row_slot < 4) & (expert == 1)
    on = jnp.concatenate([main_on.astype(jnp.float32), rest_on.astype(jnp.float32)], axis=0) > 0.5
    across = (((1,), (1,)), ((), ()))
    down = (((0,), (0,)), ((), ()))

    def dot(a, b, dims=(((1,), (0,)), ((), ()))):
        return lax.dot_general(a, b, dims, preferred_element_type=jnp.float32)

    def up_rows(a, amount):
        return pltpu.roll(a, count - amount, 0)

    def dot_copy(device, landing, sender):
        return pltpu.make_async_remote_copy(
            src_ref=dots.at[position(device)],
            dst_ref=held.at[landing],
            send_sem=dot_send.at[device],
            recv_sem=dot_recv.at[sender],
            device_id={"expert": device},
            device_id_type=MESH,
        )

    def half_rows(column, finish):
        rows = pl.ds(pl.multiple_of(column * count, count), count)
        rest = packed[rows, 2 * width : 2 * width + half]

        def stacked(start, size, rest_start):
            return jnp.concatenate(
                [packed[rows, start : start + size], rest[:, rest_start : rest_start + size]], axis=0
            )

        pre_low = dot(stacked(0, half, 0), joined_ref[:half, :])
        pre_high = dot(stacked(half, half, 0), joined_ref[half:, :])
        back_low = dot(stacked(width, half, 0), down_ref[:, :half], across)
        back_high = dot(stacked(width + half, half, 0), down_ref[:, half:], across)
        pre = jnp.concatenate(
            [pre_low[:count] + pre_high[:count], pre_low[count:] + up_rows(pre_high[count:], 4)], axis=0
        )
        back = jnp.concatenate(
            [
                back_low[:count] + back_high[:count],
                up_rows(back_low[count:], 8) + up_rows(back_high[count:], 12),
            ],
            axis=0,
        )
        gains = packed[rows, 2 * width + half :].astype(jnp.float32)
        gain = jnp.where(on, jnp.concatenate([gains[:, 0:1], gains[:, 64:65]], axis=0), 0.0)
        pre_gate, pre_up = pre[:, :blk], pre[:, blk:]
        sigma = jax.nn.sigmoid(pre_gate)
        hidden = (pre_gate * sigma * pre_up).astype(jnp.bfloat16).astype(jnp.float32)
        products = jnp.where(on, jnp.sum(hidden * back, axis=1, keepdims=True), 0.0)
        scaled = gain * hidden
        d_hidden = gain * back
        d_gate = d_hidden * pre_up * sigma * (1.0 + pre_gate * (1.0 - sigma))
        d_up = d_hidden * pre_gate * sigma
        d_joined = jnp.concatenate([d_gate, d_up], axis=1)
        wide_lane = lax.broadcasted_iota(jnp.int32, (count, 128), 1)
        dots[pl.ds(column * 2 * depth, 2 * depth)] = jnp.where(
            wide_lane < 64, products[:count], products[count:]
        ).reshape(2 * depth, ROWS, 128)

        def send(number, carry):
            device = place(number // 2, column, lax.rem(number, 2))
            pl.when(device != me)(lambda: dot_copy(device, me, me).start())
            return carry

        lax.fori_loop(0, 2 * depth, send, 0)

        stores = []
        for part in range(2):
            d_rest = pltpu.roll(d_joined[count:], 4 * part, 0) if part else d_joined[count:]
            d_rows = jnp.concatenate([d_joined[:count], d_rest], axis=0).astype(jnp.bfloat16)
            scaled_rows = jnp.concatenate(
                [scaled[:count], pltpu.roll(scaled[count:], 8 + 4 * part, 0)], axis=0
            ).astype(jnp.bfloat16)
            tile = 512
            for start in range(0, half, tile):
                at = part * half + start
                here = slice(at, at + tile)
                grad = dot(stacked(at, tile, start), d_rows, down)
                grad_d = dot(scaled_rows, stacked(width + at, tile, start), down)
                if finish:
                    grad_joined[here, :] = (sum_joined[here, :] + grad).astype(jnp.bfloat16)
                    grad_down[:, here] = (sum_down[:, here] + grad_d).astype(jnp.bfloat16)
                else:
                    sum_joined[here, :] = grad
                    sum_down[:, here] = grad_d
            if finish:
                block = pl.ds(part * half, half)
                for number, (source, target) in enumerate(
                    (
                        (grad_joined.at[block, 0:blk], gate_out.at[block, :]),
                        (grad_joined.at[block, blk : 2 * blk], up_out.at[block, :]),
                        (grad_down.at[:, block], down_out.at[:, block]),
                    )
                ):
                    store = pltpu.make_async_copy(source, target, store_sem.at[part * 3 + number])
                    store.start()
                    stores.append(store)
        return stores

    early("start")
    for load in loads[2:]:
        load.wait()
    sibling(y)
    half_rows(y, False)
    held[me] = dots[position(me)]
    late("start")
    sibling(1 - y)
    stores = half_rows(1 - y, True)

    each_other(lambda device: dot_copy(device, device, device).wait_recv())
    total = held[0]
    for device in range(1, devices):
        total = total + held[device]
    ids = ids_ref[...]
    first, second, rest_hot, _, slot = slot_tables(ids, ids)
    total_main, extra = total[:, 0:1], total[:, 64:65]
    low = jnp.sum(first * total_main, axis=0, keepdims=True)
    high = jnp.sum(second * total_main + jnp.where(slot < 4, rest_hot * extra, 0.0), axis=0, keepdims=True)
    route_out[...] = jnp.where(ids == 0, low, jnp.where(ids == 1, high, 0.0))
    each_other(lambda device: dot_copy(device, me, me).wait_send())
    for piece in range(pieces):
        own_piece(piece, "wait_send")
    early("wait_send")
    late("wait_send")
    for store in stores:
        store.wait()


def write_kernel(a_in, b_in, c_in, route_in, a_out, b_out, c_out, route_out, a, b, c, load_sem, store_sem):
    loads, stores = [], []
    for number, (source, through, target) in enumerate(((a_in, a, a_out), (b_in, b, b_out), (c_in, c, c_out))):
        rows = source.shape[0] // 2
        for part in range(2):
            block = pl.ds(part * rows, rows)
            loads.append(
                pltpu.make_async_copy(source.at[block], through.at[block], load_sem.at[number, part])
            )
            stores.append(
                pltpu.make_async_copy(through.at[block], target.at[block], store_sem.at[number, part])
            )
    for load in loads:
        load.start()
    route_out[...] = route_in[...]
    for load, store in zip(loads, stores):
        load.wait()
        store.start()
    for store in stores:
        store.wait()


def per_device_gathered(
    tokens, grad_out, expert_ids, route_weight, block_expert, gate_blocks, up_blocks, down_blocks
):
    devices = lax.axis_size("expert")
    count, width = tokens.shape
    blk = gate_blocks.shape[2]
    ids, weights = expert_ids.T, route_weight.T
    total = 2 * width + width // 2 + 128
    pieces = 3
    vmem = pl.BlockSpec(memory_space=pltpu.VMEM)
    anywhere = pl.BlockSpec(memory_space=pl.ANY)
    grad_gate, grad_up, grad_down, route_grad = pl.pallas_call(
        functools.partial(fused_kernel, pieces),
        out_shape=(
            jax.ShapeDtypeStruct((width, blk), jnp.bfloat16),
            jax.ShapeDtypeStruct((width, blk), jnp.bfloat16),
            jax.ShapeDtypeStruct((blk, width), jnp.bfloat16),
            jax.ShapeDtypeStruct(ids.shape, jnp.float32),
        ),
        in_specs=[pl.BlockSpec(memory_space=pltpu.SMEM), vmem, vmem] + [anywhere] * 5,
        out_specs=(anywhere, anywhere, anywhere, vmem),
        scratch_shapes=[
            pltpu.VMEM((count, width), jnp.bfloat16),
            pltpu.VMEM((count, width), jnp.bfloat16),
            pltpu.VMEM((width, 2 * blk), jnp.bfloat16),
            pltpu.VMEM((blk, width), jnp.bfloat16),
            pltpu.VMEM((devices * ROWS, total), jnp.bfloat16),
            pltpu.VMEM((width, 2 * blk), jnp.bfloat16),
            pltpu.VMEM((blk, width), jnp.bfloat16),
            pltpu.VMEM((width, 2 * blk), jnp.float32),
            pltpu.VMEM((blk, width), jnp.float32),
            pltpu.VMEM((devices, ROWS, 128), jnp.float32),
            pltpu.VMEM((devices, ROWS, 128), jnp.float32),
            pltpu.SemaphoreType.DMA((5,)),
            pltpu.SemaphoreType.DMA((6,)),
            pltpu.SemaphoreType.DMA((4, devices, pieces)),
            pltpu.SemaphoreType.DMA((devices, pieces)),
            pltpu.SemaphoreType.DMA((devices,)),
            pltpu.SemaphoreType.DMA((devices,)),
        ],
        compiler_params=pltpu.CompilerParams(
            collective_id=0, has_side_effects=True, vmem_limit_bytes=58 * 1024 * 1024
        ),
        name="layer_backward",
    )(block_expert, ids, weights, tokens, grad_out, gate_blocks[0], up_blocks[0], down_blocks[0])
    results = (grad_gate, grad_up, grad_down)
    grad_gate, grad_up, grad_down, route_grad = pl.pallas_call(
        write_kernel,
        out_shape=tuple(jax.ShapeDtypeStruct(a.shape, a.dtype) for a in (*results, route_grad)),
        in_specs=[anywhere] * 3 + [vmem],
        out_specs=(anywhere,) * 3 + (vmem,),
        scratch_shapes=[pltpu.VMEM(a.shape, a.dtype) for a in results]
        + [pltpu.SemaphoreType.DMA((3, 2)), pltpu.SemaphoreType.DMA((3, 2))],
        compiler_params=pltpu.CompilerParams(vmem_limit_bytes=58 * 1024 * 1024),
        name="write_results",
    )(*results, route_grad)
    return (grad_gate[None], grad_up[None], grad_down[None], route_grad.T)


def solution(mesh):
    body = per_device_gathered if mesh.shape["expert"] == 16 else per_device
    return jax.shard_map(
        body,
        mesh=mesh,
        in_specs=(
            P(("groups", "expert"), None),
            P(("groups", "expert"), None),
            P(("groups", "expert"), None),
            P(("groups", "expert"), None),
            P(),
            P("expert", None, None),
            P("expert", None, None),
            P("expert", None, None),
        ),
        out_specs=(
            P(("groups", "expert"), None, None),
            P(("groups", "expert"), None, None),
            P(("groups", "expert"), None, None),
            P(("groups", "expert"), None),
        ),
        check_vma=False,
    )
```
